32 devices in a mesh: section: 4 (over y, x), dp: 8 (over z, core).
Axes of the slice: x: 2, y: 2, z: 4, core: 2. Of those that a mesh axis runs over, the one named last changes fastest.
Arguments:
- enter_a: bfloat16 [4, 1024, 7168], P('section', 'dp'), may hold values from -6 to 6
- enter_b: bfloat16 [4, 1024, 7168], P('section', 'dp'), may hold values from -6 to 6
- cotan_a: bfloat16 [4, 1024, 7168], P('section', 'dp'), may hold values from -6 to 6
- cotan_b: bfloat16 [4, 1024, 7168], P('section', 'dp'), may hold values from -6 to 6
- saved_a: bfloat16 [2, 4, 1024, 7168], P(None, 'section', 'dp'), may hold values from -6 to 6
- saved_b: bfloat16 [2, 4, 1024, 7168], P(None, 'section', 'dp'), may hold values from -6 to 6
- norm_gain: float32 [4, 7168], P('section'), may hold values from 0.1 to 1.9
- w_down: bfloat16 [4, 7168, 256], P('section', 'dp'), may hold values from -0.0625 to 0.0625
- latent_gain: float32 [4, 256], P('section'), may hold values from 0.1 to 1.9
- w_up: bfloat16 [4, 256, 7168], P('section', None, 'dp'), may hold values from -0.375 to 0.375
Outputs:
- out_a: bfloat16 [4, 1024, 7168], P('section', 'dp')
- out_b: bfloat16 [4, 1024, 7168], P('section', 'dp')
- back_a: bfloat16 [4, 1024, 7168], P('section', 'dp')
- back_b: bfloat16 [4, 1024, 7168], P('section', 'dp')
- grad_norm_gain: float32 [4, 7168], P('section', 'dp')
- grad_down: float32 [4, 7168, 256], P('section', 'dp')
- grad_latent_gain: float32 [4, 256], P('section', 'dp')
- grad_up: float32 [4, 256, 7168], P('section', None, 'dp')
The draws below stay inside these ranges and needn't reach their ends.
All inputs are finite; a program needn't handle non-finite values.
Results may differ from the reference program's by a relative error of at most 0.035.
Values may be sent and summed in bfloat16 or wider, within the bound.
A program may use at most 192 MiB of HBM per device.

```python
import jax
import jax.numpy as jnp
from jax import lax

D = 7168
R = 256
TOK_DEV = 128
TICKS = 2
LAYERS = 4
TOKENS = 1024
N_SECTION = 4
N_DP = 8


def spiked(entries, stream_key, source, target, shards_of, factor):
    def block_of(axis_at):
        return (jnp.arange(entries.shape[axis_at]) // (entries.shape[axis_at] // shards_of)).reshape((-1,) + (1,) * (entries.ndim - 1 - axis_at))

    near = jax.random.permutation(stream_key, shards_of)[block_of(target)]
    second = (block_of(target) + shards_of // 2) % shards_of
    return jnp.where((block_of(source) == near) | (block_of(source) == second), factor * entries, entries)


def levels(stream_key, dims, shards, low, top_value):
    level, own = 1.0, jax.random.fold_in(stream_key, 6)
    for axis_at, shards_of in shards:
        heights = jnp.exp(jax.random.uniform(jax.random.fold_in(own, axis_at), (shards_of,), jnp.float32, low / len(shards), top_value / len(shards)))
        level = level * jnp.repeat(heights, dims[axis_at] // shards_of).reshape([-1 if axis == axis_at else 1 for axis in range(len(dims))])
    return level


def noise(own_key, dims, deviation, bound, cuts=(), kind=jnp.bfloat16):
    array = deviation * jax.random.normal(own_key, dims, jnp.float32)
    if cuts:
        array = array * levels(own_key, dims, cuts, -0.22, 0.18)
    return jnp.clip(array, -bound, bound).astype(kind)


def gaussian_with(rng, extent, width, reach, shards, heavy, kind=jnp.bfloat16):
    values = width * jax.random.normal(rng, extent, jnp.float32)
    if shards:
        values = values * levels(rng, extent, shards, -0.22, 0.18)
    return jnp.clip(spiked(values, jax.random.fold_in(rng, 3), *heavy), -reach, reach).astype(kind)


def setup_inputs(seed: int = 0) -> dict:
    streams_of = jax.random.split(jax.random.key(seed), 11)
    enter_a = noise(streams_of[0], (LAYERS, TOKENS, D), 1.0, 6.0, ((0, 4), (1, 8)))
    enter_b = noise(streams_of[1], (LAYERS, TOKENS, D), 1.0, 6.0, ((0, 4), (1, 8)))
    cotan_a = noise(streams_of[2], (LAYERS, TOKENS, D), 1.0, 6.0, ((0, 4), (1, 8)))
    cotan_b = noise(streams_of[3], (LAYERS, TOKENS, D), 1.0, 6.0, ((0, 4), (1, 8)))
    saved_a = gaussian_with(streams_of[4], (TICKS, LAYERS, TOKENS, D), 1.0, 6.0, ((1, 4), (2, 8)), (2, 3, 8, 2.0))
    saved_b = gaussian_with(streams_of[5], (TICKS, LAYERS, TOKENS, D), 1.0, 6.0, ((1, 4), (2, 8)), (2, 3, 8, 2.0))
    norm_gain = jnp.clip(1.0 + 0.18 * jax.random.normal(streams_of[6], (LAYERS, D), jnp.float32), 0.1, 1.9)
    w_down = noise(streams_of[7], (LAYERS, D, R), D ** -0.5, 0.0625, ((0, 4), (1, 8)))
    latent_gain = jnp.clip(1.0 + 0.18 * jax.random.normal(streams_of[8], (LAYERS, R), jnp.float32), 0.1, 1.9)
    w_up = noise(streams_of[9], (LAYERS, R, D), R ** -0.5, 0.375, ((0, 4), (2, 8)))
    return dict(enter_a=enter_a, enter_b=enter_b, cotan_a=cotan_a, cotan_b=cotan_b, saved_a=saved_a, saved_b=saved_b, norm_gain=norm_gain, w_down=w_down, latent_gain=latent_gain, w_up=w_up)


def layer(x, norm_gain, w_down, latent_gain, w_up):
    xf = x.astype(jnp.float32)
    normed = (xf * lax.rsqrt(lax.optimization_barrier(jnp.mean(xf * xf, axis=-1, keepdims=True)) + 1e-06) * norm_gain).astype(jnp.bfloat16)
    latent = jnp.dot(normed, w_down, preferred_element_type=jnp.float32)
    scaled = (latent * lax.rsqrt(lax.optimization_barrier(jnp.mean(latent * latent, axis=-1, keepdims=True)) + 1e-06) * latent_gain).astype(jnp.bfloat16)
    return (xf + jnp.dot(scaled, w_up, preferred_element_type=jnp.float32)).astype(jnp.bfloat16)

def layer_grads(x, cotangent, weights):
    _, pull = jax.vjp(layer, x, *weights)
    return pull(cotangent)

def block_grads(x, cotangent, weights):
    blocks_x = x.reshape(N_DP, TOK_DEV, D)
    blocks_c = cotangent.reshape(N_DP, TOK_DEV, D)
    result = jax.vmap(lambda a, c: layer_grads(a, c, weights))(blocks_x, blocks_c)
    back = result[0].reshape(N_DP * TOK_DEV, D)
    grads = tuple((g.astype(jnp.float32) for g in result[1:]))
    return (back, grads)

def rounded(value):
    narrow = lax.optimization_barrier(value.astype(jnp.bfloat16))
    return narrow.astype(jnp.float32)

def reference(enter_a, enter_b, cotan_a, cotan_b, saved_a, saved_b, norm_gain, w_down, latent_gain, w_up):
    sections = N_SECTION

    def weights(level):
        return (norm_gain[level], w_down[level], latent_gain[level], w_up[level])

    def empty_grads():
        return (jnp.zeros((N_DP, D), jnp.float32), jnp.zeros((N_DP, D, R), jnp.float32), jnp.zeros((N_DP, R), jnp.float32), jnp.zeros((N_DP, R, D), jnp.float32))
    accum_a = [empty_grads() for level in range(sections)]
    accum_b = [empty_grads() for level in range(sections)]
    zero_rows = jnp.zeros_like(enter_a[0])
    cur_a = [enter_a[s] for s in range(sections)]
    cur_b = [enter_b[s] for s in range(sections)]
    cur_ga = [cotan_a[s] for s in range(sections)]
    cur_gb = [cotan_b[s] for s in range(sections)]
    for tick in range(TICKS):
        out_a = [layer(cur_a[s], *weights(s)) for s in range(sections)]
        out_b = [layer(cur_b[s], *weights(sections - 1 - s)) for s in range(sections)]
        back_a = []
        back_b = []
        for s in range(sections):
            back, grads = block_grads(saved_a[tick, s], cur_ga[s], weights(s))
            back_a.append(back)
            accum_a[s] = tuple((p + q for p, q in zip(accum_a[s], grads)))
        for s in range(sections):
            level = sections - 1 - s
            back, grads = block_grads(saved_b[tick, s], cur_gb[s], weights(level))
            back_b.append(back)
            accum_b[level] = tuple((p + q for p, q in zip(accum_b[level], grads)))
        if tick < TICKS - 1:
            cur_a = [zero_rows] + out_a[:-1]
            cur_b = out_b[1:] + [zero_rows]
            cur_ga = back_a[1:] + [zero_rows]
            cur_gb = [zero_rows] + back_b[:-1]
    totals = []
    for k in range(4):
        per_layer = [lax.optimization_barrier(jnp.sum(rounded(accum_a[level][k]) + rounded(accum_b[level][k]), axis=0)) for level in range(sections)]
        totals.append(jnp.stack(per_layer))
    return (jnp.stack(out_a), jnp.stack(out_b), jnp.stack(back_a), jnp.stack(back_b), totals[0], totals[1], totals[2], totals[3])
```

```python
import functools

import jax
import jax.numpy as jnp
from jax import lax
from jax.experimental import pallas as pl
from jax.experimental.pallas import tpu as pltpu
from jax.sharding import PartitionSpec as P

TICKS = 2
MESH = pl.DeviceIdType.MESH
BF16 = jnp.bfloat16
F32 = jnp.float32


def place():
    s, d = lax.axis_index("section"), lax.axis_index("dp")
    return s, d, lax.div(d, 2), lax.rem(d, 2)


def greet(sections, chips):
    s, d, z, c = place()
    barrier = pltpu.get_barrier_semaphore()

    def hello(section, index):
        pl.semaphore_signal(barrier, inc=1, device_id=(section, index), device_id_type=MESH)

    hello(sections - 1 - s, d)
    hello(s, d + 1 - 2 * c)

    @pl.when(z > 0)
    def _():
        hello(s, d - 2)

    @pl.when(z < chips - 1)
    def _():
        hello(s, d + 2)

    pl.semaphore_wait(barrier, 2 + jnp.minimum(z, 1) + jnp.minimum(chips - 1 - z, 1))


def down_at(full, e, rows):
    return full.at[pl.ds(pl.multiple_of(e * rows, 16), rows), :]


def up_at(full, e, columns):
    if len(full.shape) == 3:
        return full.at[e]
    return full.at[:, pl.ds(pl.multiple_of(e * columns, 128), columns)]


def remote(src, dst, send, recv, device):
    return pltpu.make_async_remote_copy(
        src_ref=src, dst_ref=dst, send_sem=send, recv_sem=recv, device_id=device, device_id_type=MESH
    )


def gather_kernel(
    sections, chips, wd, wu, gains, owd, owu, mwd, mwu, mgains, sems, local_sems, gain_sems
):
    s, d, z, c = place()
    width = wd.shape[0]
    mirror = (sections - 1 - s, d)
    sibling = (s, d + 1 - 2 * c)
    right, left = (s, d + 2), (s, d - 2)
    greet(sections, chips)

    def slot(full, p, chip, core):
        return (down_at, up_at)[p](full[p], chip * 2 + core, width)

    own, mir, shard = (owd, owu), (mwd, mwu), (wd, wu)

    def at(kind, p, chip):
        return sems.at[kind, p, chip]

    def line_copy(p, chip, src, kind, device):
        return remote(src, slot(own, p, chip, c), at(kind, p, chip), at(0, p, chip), device)

    def sibling_copy(p, chip, src):
        return remote(src, slot(own, p, chip, c), at(3, p, chip), at(4, p, chip), sibling)

    def mirror_copy(p, chip, src):
        return remote(src, slot(mir, p, chip, c), at(5, p, chip), at(6, p, chip), mirror)

    def mirror_sibling_copy(p, chip):
        block = slot(mir, p, chip, c)
        return remote(block, block, at(7, p, chip), at(8, p, chip), sibling)

    gain_copy = remote(gains, mgains, gain_sems.at[0], gain_sems.at[1], mirror)
    for p in range(2):
        pltpu.make_async_copy(shard[p], slot(own, p, z, c), local_sems.at[p]).start()

        @pl.when(z < chips - 1)
        def _():
            line_copy(p, z, shard[p], 1, right).start()

        @pl.when(z > 0)
        def _():
            line_copy(p, z, shard[p], 2, left).start()

        mirror_copy(p, z, shard[p]).start()
        sibling_copy(p, z, shard[p]).start()
    gain_copy.start()

    def pass_mirror(k):
        for p in range(2):
            for chip in (z - k, z + k)[: 1 if k == 0 else 2]:

                @pl.when((chip >= 0) & (chip < chips))
                def _():
                    mirror_copy(p, chip, slot(mir, p, chip, c)).wait_recv()
                    mirror_sibling_copy(p, chip).start()

    for k in range(1, chips):
        for p in range(2):

            @pl.when(z - k >= 0)
            def _():
                block = slot(own, p, z - k, c)
                line_copy(p, z - k, block, 1, right).wait_recv()

                @pl.when(z < chips - 1)
                def _():
                    line_copy(p, z - k, block, 1, right).start()

                mirror_copy(p, z - k, block).start()
                sibling_copy(p, z - k, block).start()

            @pl.when(z + k < chips)
            def _():
                block = slot(own, p, z + k, c)
                line_copy(p, z + k, block, 2, left).wait_recv()

                @pl.when(z > 0)
                def _():
                    line_copy(p, z + k, block, 2, left).start()

                mirror_copy(p, z + k, block).start()
                sibling_copy(p, z + k, block).start()

        pass_mirror(k - 1)
    pass_mirror(chips - 1)

    for p in range(2):
        pltpu.make_async_copy(shard[p], slot(own, p, z, c), local_sems.at[p]).wait()
        for chip in range(chips):
            theirs = slot(own, p, chip, 1 - c)
            remote(theirs, theirs, at(3, p, chip), at(4, p, chip), sibling).wait()
            mirror_copy(p, chip, slot(own, p, chip, c)).wait_send()
            theirs = slot(mir, p, chip, 1 - c)
            remote(theirs, theirs, at(7, p, chip), at(8, p, chip), sibling).wait()

            @pl.when((chip <= z) & (z < chips - 1))
            def _():
                line_copy(p, chip, slot(own, p, chip, c), 1, right).wait_send()

            @pl.when((chip >= z) & (z > 0))
            def _():
                line_copy(p, chip, slot(own, p, chip, c), 2, left).wait_send()

    gain_copy.wait()


def gather(sections, n_dp, wd, wu, gains):
    width, rank = wd.shape
    up_shape = (rank, n_dp * width) if width % 128 == 0 else (n_dp, rank, width)
    down = jax.ShapeDtypeStruct((n_dp * width, rank), wd.dtype)
    up = jax.ShapeDtypeStruct(up_shape, wu.dtype)
    chips = n_dp // 2
    owd, owu, mwd, mwu, mgains = pl.pallas_call(
        functools.partial(gather_kernel, sections, chips),
        out_shape=(down, up, down, up, jax.ShapeDtypeStruct(gains.shape, gains.dtype)),
        in_specs=[pl.BlockSpec(memory_space=pl.ANY)] * 3,
        out_specs=(pl.BlockSpec(memory_space=pl.ANY),) * 5,
        scratch_shapes=[
            pltpu.SemaphoreType.DMA((9, 2, chips)),
            pltpu.SemaphoreType.DMA((2,)),
            pltpu.SemaphoreType.DMA((2,)),
        ],
        compiler_params=pltpu.CompilerParams(
            collective_id=0, has_side_effects=True, vmem_limit_bytes=56 * 2**20
        ),
        name="gather_weights",
    )(wd, wu, gains)

    def whole(v):
        return v if v.ndim == 2 else v.transpose(1, 0, 2).reshape(rank, n_dp * width)

    return owd, whole(owu), mwd, whole(mwu), mgains


def reduce_kernel(sections, chips, ad, au, asm, bd, bu, bsm, od, ou, osm, *scratch):
    s, d, z, c = place()
    width = od.shape[0]
    mirror = (sections - 1 - s, d)
    sibling = (s, d + 1 - 2 * c)
    right, left = (s, d + 2), (s, d - 2)
    mine_a, mine_b, got_a, got_b, crossed, from_left, from_right = (
        scratch[3 * i : 3 * i + 3] for i in range(7)
    )
    sems = scratch[21]
    a, b, out = (ad, au, asm), (bd, bu, bsm), (od, ou, osm)

    def part(full, p, chip, core):
        e = chip * 2 + core
        if p == 0:
            return down_at(full[0], e, width)
        if p == 1:
            return up_at(full[1], e, width)
        return full[2].at[e]

    def at(kind, p, chip):
        return sems.at[kind, p, chip]

    def load(p, chip, full, mine, kind):
        return pltpu.make_async_copy(part(full, p, chip, c), mine[p].at[chip], at(kind, p, chip))

    def swap(p, chip, full, got, kind):
        return remote(
            part(full, p, chip, 1 - c), got[p].at[chip], at(kind, p, chip), at(kind + 1, p, chip), sibling
        )

    def cross(p, chip):
        return remote(mine_b[p].at[chip], crossed[p].at[chip], at(6, p, chip), at(7, p, chip), mirror)

    def to_right(p, chip):
        return remote(mine_a[p].at[chip], from_left[p].at[chip], at(8, p, chip), at(9, p, chip), right)

    def to_left(p, chip):
        return remote(mine_a[p].at[chip], from_right[p].at[chip], at(10, p, chip), at(11, p, chip), left)

    def add(p, chip, dst, terms):
        rows = terms[0][p].shape[1]
        step = rows if p == 2 else rows // 8 if rows % 128 == 0 else rows // 7

        def body(i, carry):
            at_rows = pl.ds(pl.multiple_of(i * step, 8 if p == 2 else 16), step)
            total = terms[0][p][chip, at_rows, :].astype(F32)
            for term in terms[1:]:
                total = total + term[p][chip, at_rows, :].astype(F32)
            if dst is out:
                dst[p][at_rows, :] = total
            else:
                dst[p][chip, at_rows, :] = total.astype(dst[p].dtype)
            return carry

        lax.fori_loop(0, rows // step, body, 0)

    def each(k, do):
        if k == 0:
            do(z, 0)
        else:

            @pl.when(z + k < chips)
            def _():
                do(z + k, 1)

            @pl.when(z - k >= 0)
            def _():
                do(z - k, -1)

    greet(sections, chips)
    far_first = list(range(chips - 1, -1, -1))
    for full, mine, got, kind, local in ((b, mine_b, got_b, 4, 1), (a, mine_a, got_a, 2, 0)):
        for k in far_first:

            def begin(chip, side):
                for p in range(3):
                    swap(p, chip, full, got, kind).start()
                    load(p, chip, full, mine, local).start()

            each(k, begin)
    for full, mine, got, kind, local in ((b, mine_b, got_b, 4, 1), (a, mine_a, got_a, 2, 0)):
        for k in far_first:

            def pair(chip, side):
                for p in range(3):
                    swap(p, chip, full, got, kind).wait_recv()
                    load(p, chip, full, mine, local).wait()
                    add(p, chip, mine, (mine, got))
                    if local == 1:
                        cross(p, chip).start()

            each(k, pair)

    for k in far_first:

        def onward(chip, side):
            for p in range(3):
                cross(p, chip).wait_recv()
                if side == 1:

                    @pl.when(z > 0)
                    def _():
                        to_right(p, chip).wait_recv()
                        add(p, chip, mine_a, (mine_a, crossed, from_left))

                    @pl.when(z == 0)
                    def _():
                        add(p, chip, mine_a, (mine_a, crossed))

                    to_right(p, chip).start()
                elif side == -1:

                    @pl.when(z < chips - 1)
                    def _():
                        to_left(p, chip).wait_recv()
                        add(p, chip, mine_a, (mine_a, crossed, from_right))

                    @pl.when(z == chips - 1)
                    def _():
                        add(p, chip, mine_a, (mine_a, crossed))

                    to_left(p, chip).start()
                else:

                    @pl.when(z > 0)
                    def _():
                        to_right(p, chip).wait_recv()

                    @pl.when(z < chips - 1)
                    def _():
                        to_left(p, chip).wait_recv()

                    @pl.when(z == 0)
                    def _():
                        add(p, chip, out, (mine_a, crossed, from_right))

                    @pl.when(z == chips - 1)
                    def _():
                        add(p, chip, out, (mine_a, crossed, from_left))

                    @pl.when((z > 0) & (z < chips - 1))
                    def _():
                        add(p, chip, out, (mine_a, crossed, from_left, from_right))

        each(k, onward)

    for k in far_first:

        def finish(chip, side):
            for p in range(3):
                swap(p, chip, a, got_a, 2).wait_send()
                swap(p, chip, b, got_b, 4).wait_send()
                cross(p, chip).wait_send()
                if side == 1:
                    to_right(p, chip).wait_send()
                elif side == -1:
                    to_left(p, chip).wait_send()

        each(k, finish)


def reduce_grads(sections, n_dp, grads_a, grads_b):
    total, rank = grads_a[0].shape
    width = total // n_dp
    chips = n_dp // 2

    def prepared(grads):
        norm, down, latent, up = grads[2], grads[0], grads[3], grads[1]
        if width % 128:
            up = up.reshape(rank, n_dp, width).transpose(1, 0, 2)
        small = jnp.concatenate([norm.reshape(n_dp, width), latent.reshape(n_dp, rank // n_dp)], axis=1)
        small = jnp.pad(small, ((0, 0), (0, 1024 - small.shape[1]))).reshape(n_dp, 8, 128)
        return down, up, small

    blocks = [
        pltpu.VMEM((chips, width, rank), BF16),
        pltpu.VMEM((chips, rank, width), BF16),
        pltpu.VMEM((chips, 8, 128), F32),
    ]
    down, up, small = pl.pallas_call(
        functools.partial(reduce_kernel, sections, chips),
        out_shape=(
            jax.ShapeDtypeStruct((width, rank), F32),
            jax.ShapeDtypeStruct((rank, width), F32),
            jax.ShapeDtypeStruct((8, 128), F32),
        ),
        in_specs=[pl.BlockSpec(memory_space=pl.ANY)] * 6,
        out_specs=(pl.BlockSpec(memory_space=pltpu.VMEM),) * 3,
        scratch_shapes=blocks * 7 + [pltpu.SemaphoreType.DMA((12, 3, chips))],
        compiler_params=pltpu.CompilerParams(
            collective_id=1, has_side_effects=True, vmem_limit_bytes=56 * 2**20
        ),
        name="reduce_grads",
    )(*prepared(grads_a), *prepared(grads_b))
    flat = small.reshape(1024)
    return flat[:width], down, flat[width : width + rank // n_dp], up


def from_behind(block, axis, distance):
    devices = range(lax.axis_size(axis))
    route = [(i - distance, i) for i in devices if i - distance in devices]
    return lax.ppermute(block, axis, route)


def dot(p, q, contract):
    return lax.dot_general(p, q, (contract, ((), ())), preferred_element_type=F32)


def inner(x, gain, wd, latent_gain):
    xf = x.astype(F32)
    r = lax.rsqrt(jnp.mean(xf * xf, axis=-1, keepdims=True) + 1e-06)
    normed = (xf * r * gain).astype(BF16)
    latent = dot(normed, wd, ((1,), (0,)))
    rl = lax.rsqrt(jnp.mean(latent * latent, axis=-1, keepdims=True) + 1e-06)
    scaled = (latent * rl * latent_gain).astype(BF16)
    return r, normed, latent, rl, scaled


def forward(x, weights):
    gain, wd, latent_gain, wu = weights
    scaled = inner(x, gain, wd, latent_gain)[4]
    return (x.astype(F32) + dot(scaled, wu, ((1,), (0,)))).astype(BF16)


def backward(x, g, saved, weights):
    gain, wd, latent_gain, wu = weights
    r, normed, latent, rl, scaled = saved
    d_scaled = dot(g, wu, ((1,), (1,)))
    d_latent_gain = jnp.sum(d_scaled * latent * rl, axis=0)
    d_hat = d_scaled * latent_gain
    d_latent = rl * (d_hat - latent * (rl * rl * jnp.mean(d_hat * latent, axis=-1, keepdims=True)))
    d_latent = d_latent.astype(BF16)
    d_down = dot(normed, d_latent, ((0,), (0,)))
    d_up = dot(scaled, g, ((0,), (0,)))
    d_normed = dot(d_latent, wd, ((1,), (1,))).astype(BF16).astype(F32)
    xf = x.astype(F32)
    d_gain = jnp.sum(d_normed * (xf * r), axis=0)
    d_unit = d_normed * gain
    back = g.astype(F32) + r * (
        d_unit - xf * (r * r * jnp.mean(d_unit * xf, axis=-1, keepdims=True))
    )
    return back.astype(BF16), (d_down, d_up, d_gain, d_latent_gain)


def body(
    enter_a, enter_b, cotan_a, cotan_b, saved_a, saved_b, norm_gain, w_down, latent_gain, w_up
):
    sections, n_dp = lax.axis_size("section"), lax.axis_size("dp")
    total, rank = norm_gain.shape[1], latent_gain.shape[1]
    gains = jnp.concatenate([norm_gain[0], latent_gain[0]])
    gains = jnp.pad(gains, (0, -gains.shape[0] % 1024)).reshape(-1, 128)
    owd, owu, mwd, mwu, mgains = gather(sections, n_dp, w_down[0], w_up[0], gains)
    mgains = mgains.reshape(-1)
    own = (norm_gain[0], owd, latent_gain[0], owu)
    mir = (mgains[:total], mwd, mgains[total : total + rank], mwu)

    def step(x, saved_x, g, weights):
        kept = inner(saved_x, weights[0], weights[1], weights[2])
        back, grads = backward(saved_x, g, kept, weights)
        return forward(x, weights), back, grads

    out_a, back_a, sum_a = step(enter_a[0], saved_a[0, 0], cotan_a[0], own)
    grad_a = from_behind(back_a, "section", -1)
    state_a = from_behind(out_a, "section", 1)
    out_b, back_b, sum_b = step(enter_b[0], saved_b[0, 0], cotan_b[0], mir)
    grad_b = from_behind(back_b, "section", 1)
    state_b = from_behind(out_b, "section", -1)

    out_a, back_a, more_a = step(state_a, saved_a[1, 0], grad_a, own)
    out_b, back_b, more_b = step(state_b, saved_b[1, 0], grad_b, mir)

    def summed(first, second):
        both = [p + q for p, q in zip(first, second)]
        rounded = [v.astype(BF16) for v in both]
        return rounded[0], rounded[1], rounded[2].astype(F32), rounded[3].astype(F32)

    norm, down, latent, up = reduce_grads(
        sections, n_dp, summed(sum_a, more_a), summed(sum_b, more_b)
    )
    return (
        out_a[None],
        out_b[None],
        back_a[None],
        back_b[None],
        norm[None],
        down[None],
        latent[None],
        up[None],
    )


def solution(mesh):
    placed = (
        P("section", "dp", None),
        P("section", "dp", None),
        P("section", "dp", None),
        P("section", "dp", None),
        P(None, "section", "dp", None),
        P(None, "section", "dp", None),
        P("section", None),
        P("section", "dp", None),
        P("section", None),
        P("section", None, "dp"),
    )
    return jax.shard_map(
        body,
        mesh=mesh,
        in_specs=placed,
        out_specs=(
            P("section", "dp", None),
            P("section", "dp", None),
            P("section", "dp", None),
            P("section", "dp", None),
            P("section", "dp"),
            P("section", "dp", None),
            P("section", "dp"),
            P("section", None, "dp"),
        ),
        check_vma=False,
    )
```

```python
import functools

import jax
import jax.numpy as jnp
from jax import lax
from jax.experimental import pallas as pl
from jax.experimental.pallas import tpu as pltpu
from jax.sharding import PartitionSpec as P

TICKS = 2
MESH = pl.DeviceIdType.MESH
BF16 = jnp.bfloat16
F32 = jnp.float32


def place():
    s, d = lax.axis_index("section"), lax.axis_index("dp")
    return s, d, lax.div(d, 2), lax.rem(d, 2)


def greet(sections, chips):
    s, d, z, c = place()
    barrier = pltpu.get_barrier_semaphore()

    def hello(section, index):
        pl.semaphore_signal(barrier, inc=1, device_id=(section, index), device_id_type=MESH)

    hello(sections - 1 - s, d)
    hello(s, d + 1 - 2 * c)

    @pl.when(z > 0)
    def _():
        hello(s, d - 2)

    @pl.when(z < chips - 1)
    def _():
        hello(s, d + 2)

    pl.semaphore_wait(barrier, 2 + jnp.minimum(z, 1) + jnp.minimum(chips - 1 - z, 1))


def down_at(full, e, rows):
    return full.at[pl.ds(pl.multiple_of(e * rows, 16), rows), :]


def up_at(full, e, columns):
    if len(full.shape) == 3:
        return full.at[e]
    return full.at[:, pl.ds(pl.multiple_of(e * columns, 128), columns)]


def remote(src, dst, send, recv, device):
    return pltpu.make_async_remote_copy(
        src_ref=src, dst_ref=dst, send_sem=send, recv_sem=recv, device_id=device, device_id_type=MESH
    )


def gather_kernel(
    sections, chips, wd, wu, gains, owd, owu, mwd, mwu, mgains, sems, local_sems, gain_sems
):
    s, d, z, c = place()
    width = wd.shape[0]
    mirror = (sections - 1 - s, d)
    sibling = (s, d + 1 - 2 * c)
    right, left = (s, d + 2), (s, d - 2)
    greet(sections, chips)

    def slot(full, p, chip, core):
        return (down_at, up_at)[p](full[p], chip * 2 + core, width)

    own, mir, shard = (owd, owu), (mwd, mwu), (wd, wu)

    def at(kind, p, chip):
        return sems.at[kind, p, chip]

    def line_copy(p, chip, src, kind, device):
        return remote(src, slot(own, p, chip, c), at(kind, p, chip), at(0, p, chip), device)

    def sibling_copy(p, chip, src):
        return remote(src, slot(own, p, chip, c), at(3, p, chip), at(4, p, chip), sibling)

    def mirror_copy(p, chip, src):
        return remote(src, slot(mir, p, chip, c), at(5, p, chip), at(6, p, chip), mirror)

    def mirror_sibling_copy(p, chip):
        block = slot(mir, p, chip, c)
        return remote(block, block, at(7, p, chip), at(8, p, chip), sibling)

    def mirror_line_copy(chip, toward):
        kind, device = (9, right) if toward == 1 else (11, left)
        block = slot(mir, 1, chip, c)
        return remote(block, block, at(kind, 1, chip), at(kind + 1, 1, chip), device)

    gain_copy = remote(gains, mgains, gain_sems.at[0], gain_sems.at[1], mirror)
    for p in range(2):
        pltpu.make_async_copy(shard[p], slot(own, p, z, c), local_sems.at[p]).start()

        @pl.when(z < chips - 1)
        def _():
            line_copy(p, z, shard[p], 1, right).start()

        @pl.when(z > 0)
        def _():
            line_copy(p, z, shard[p], 2, left).start()

        mirror_copy(p, z, shard[p]).start()
        sibling_copy(p, z, shard[p]).start()
    gain_copy.start()

    def pass_mirror(k):
        for p in range(2):
            for side, chip in enumerate((z - k, z + k)[: 1 if k == 0 else 2]):

                @pl.when((chip >= 0) & (chip < chips))
                def _():
                    if k == 1 and p == 1:
                        mirror_line_copy(chip, 1 if side == 0 else -1).wait_recv()
                    else:
                        mirror_copy(p, chip, slot(mir, p, chip, c)).wait_recv()
                    mirror_sibling_copy(p, chip).start()

                if k == 0 and p == 1:

                    @pl.when(z < chips - 1)
                    def _():
                        mirror_line_copy(z, 1).start()

                    @pl.when(z > 0)
                    def _():
                        mirror_line_copy(z, -1).start()

    for k in range(1, chips):
        for p in range(2):

            @pl.when(z - k >= 0)
            def _():
                block = slot(own, p, z - k, c)
                line_copy(p, z - k, block, 1, right).wait_recv()

                @pl.when(z < chips - 1)
                def _():
                    line_copy(p, z - k, block, 1, right).start()

                if k > 1 or p == 0:
                    mirror_copy(p, z - k, block).start()
                sibling_copy(p, z - k, block).start()

            @pl.when(z + k < chips)
            def _():
                block = slot(own, p, z + k, c)
                line_copy(p, z + k, block, 2, left).wait_recv()

                @pl.when(z > 0)
                def _():
                    line_copy(p, z + k, block, 2, left).start()

                if k > 1 or p == 0:
                    mirror_copy(p, z + k, block).start()
                sibling_copy(p, z + k, block).start()

        pass_mirror(k - 1)
    pass_mirror(chips - 1)

    for p in range(2):
        pltpu.make_async_copy(shard[p], slot(own, p, z, c), local_sems.at[p]).wait()
        for chip in range(chips):
            theirs = slot(own, p, chip, 1 - c)
            remote(theirs, theirs, at(3, p, chip), at(4, p, chip), sibling).wait()
            if p == 0:
                mirror_copy(p, chip, slot(own, p, chip, c)).wait_send()
            else:

                @pl.when((chip != z + 1) & (chip != z - 1))
                def _():
                    mirror_copy(p, chip, slot(own, p, chip, c)).wait_send()

            theirs = slot(mir, p, chip, 1 - c)
            remote(theirs, theirs, at(7, p, chip), at(8, p, chip), sibling).wait()

            @pl.when((chip <= z) & (z < chips - 1))
            def _():
                line_copy(p, chip, slot(own, p, chip, c), 1, right).wait_send()

            @pl.when((chip >= z) & (z > 0))
            def _():
                line_copy(p, chip, slot(own, p, chip, c), 2, left).wait_send()

    @pl.when(z < chips - 1)
    def _():
        mirror_line_copy(z, 1).wait_send()

    @pl.when(z > 0)
    def _():
        mirror_line_copy(z, -1).wait_send()

    gain_copy.wait()


def gather(sections, n_dp, wd, wu, gains):
    width, rank = wd.shape
    up_shape = (rank, n_dp * width) if width % 128 == 0 else (n_dp, rank, width)
    down = jax.ShapeDtypeStruct((n_dp * width, rank), wd.dtype)
    up = jax.ShapeDtypeStruct(up_shape, wu.dtype)
    chips = n_dp // 2
    owd, owu, mwd, mwu, mgains = pl.pallas_call(
        functools.partial(gather_kernel, sections, chips),
        out_shape=(down, up, down, up, jax.ShapeDtypeStruct(gains.shape, gains.dtype)),
        in_specs=[pl.BlockSpec(memory_space=pl.ANY)] * 3,
        out_specs=(pl.BlockSpec(memory_space=pl.ANY),) * 5,
        scratch_shapes=[
            pltpu.SemaphoreType.DMA((13, 2, chips)),
            pltpu.SemaphoreType.DMA((2,)),
            pltpu.SemaphoreType.DMA((2,)),
        ],
        compiler_params=pltpu.CompilerParams(
            collective_id=0, has_side_effects=True, vmem_limit_bytes=56 * 2**20
        ),
        name="gather_weights",
    )(wd, wu, gains)

    def whole(v):
        return v if v.ndim == 2 else v.transpose(1, 0, 2).reshape(rank, n_dp * width)

    return owd, whole(owu), mwd, whole(mwu), mgains


def reduce_kernel(sections, chips, ad, au, asm, bd, bu, bsm, od, ou, osm, *scratch):
    s, d, z, c = place()
    width = od.shape[0]
    mirror = (sections - 1 - s, d)
    sibling = (s, d + 1 - 2 * c)
    right, left = (s, d + 2), (s, d - 2)
    mine_a, mine_b, got_a, got_b, crossed, from_left, from_right = (
        scratch[3 * i : 3 * i + 3] for i in range(7)
    )
    sems, left_b, right_b = scratch[21:24]
    a, b, out = (ad, au, asm), (bd, bu, bsm), (od, ou, osm)

    def part(full, p, chip, core):
        e = chip * 2 + core
        if p == 0:
            return down_at(full[0], e, width)
        if p == 1:
            return up_at(full[1], e, width)
        return full[2].at[e]

    def at(kind, p, chip):
        return sems.at[kind, p, chip]

    def load(p, chip, full, mine, kind):
        return pltpu.make_async_copy(part(full, p, chip, c), mine[p].at[chip], at(kind, p, chip))

    def swap(p, chip, full, got, kind):
        return remote(
            part(full, p, chip, 1 - c), got[p].at[chip], at(kind, p, chip), at(kind + 1, p, chip), sibling
        )

    def cross(p, chip):
        return remote(mine_b[p].at[chip], crossed[p].at[chip], at(6, p, chip), at(7, p, chip), mirror)

    def to_right(p, chip, stream=0):
        kind, mine, lands = ((8, mine_a, from_left), (12, mine_b, {1: left_b}))[stream]
        return remote(
            mine[p].at[chip], lands[p].at[chip], at(kind, p, chip), at(kind + 1, p, chip), right
        )

    def to_left(p, chip, stream=0):
        kind, mine, lands = ((10, mine_a, from_right), (14, mine_b, {1: right_b}))[stream]
        return remote(
            mine[p].at[chip], lands[p].at[chip], at(kind, p, chip), at(kind + 1, p, chip), left
        )

    def add(p, chip, dst, terms):
        rows = terms[0][p].shape[1]
        step = rows if p == 2 else rows // 8 if rows % 128 == 0 else rows // 7

        def body(i, carry):
            at_rows = pl.ds(pl.multiple_of(i * step, 8 if p == 2 else 16), step)
            total = terms[0][p][chip, at_rows, :].astype(F32)
            for term in terms[1:]:
                total = total + term[p][chip, at_rows, :].astype(F32)
            if dst is out:
                dst[p][at_rows, :] = total
            else:
                dst[p][chip, at_rows, :] = total.astype(dst[p].dtype)
            return carry

        lax.fori_loop(0, rows // step, body, 0)

    def each(k, do):
        if k == 0:
            do(z, 0)
        else:

            @pl.when(z + k < chips)
            def _():
                do(z + k, 1)

            @pl.when(z - k >= 0)
            def _():
                do(z - k, -1)

    greet(sections, chips)
    far_first = list(range(chips - 1, -1, -1))
    for full, mine, got, kind, local in ((b, mine_b, got_b, 4, 1), (a, mine_a, got_a, 2, 0)):
        for k in far_first:

            def begin(chip, side):
                for p in range(3):
                    swap(p, chip, full, got, kind).start()
                    load(p, chip, full, mine, local).start()

            each(k, begin)
    for full, mine, got, kind, local in ((b, mine_b, got_b, 4, 1), (a, mine_a, got_a, 2, 0)):
        for k in far_first:

            def pair(chip, side):
                for p in range(3):
                    swap(p, chip, full, got, kind).wait_recv()
                    load(p, chip, full, mine, local).wait()
                    add(p, chip, mine, (mine, got))
                    if local == 1 and p != 1:
                        cross(p, chip).start()

            each(k, pair)

    def pass_on(p, chip, side, stream, terms):
        mine = (mine_a, mine_b)[stream]
        lands_left = (from_left, {1: left_b})[stream]
        lands_right = (from_right, {1: right_b})[stream]
        first, last = z == 0, z == chips - 1
        if side == 1:

            @pl.when(jnp.logical_not(first))
            def _():
                to_right(p, chip, stream).wait_recv()
                add(p, chip, mine, terms + (lands_left,))

            if len(terms) > 1:

                @pl.when(first)
                def _():
                    add(p, chip, mine, terms)

            to_right(p, chip, stream).start()
        elif side == -1:

            @pl.when(jnp.logical_not(last))
            def _():
                to_left(p, chip, stream).wait_recv()
                add(p, chip, mine, terms + (lands_right,))

            if len(terms) > 1:

                @pl.when(last)
                def _():
                    add(p, chip, mine, terms)

            to_left(p, chip, stream).start()
        else:

            @pl.when(jnp.logical_not(first))
            def _():
                to_right(p, chip, stream).wait_recv()

            @pl.when(jnp.logical_not(last))
            def _():
                to_left(p, chip, stream).wait_recv()

            if stream == 0 and p == 1:
                cross(p, chip).wait_recv()
                terms = terms + (crossed,)
            dst = (out, mine_b)[stream]

            @pl.when(first)
            def _():
                add(p, chip, dst, terms + (lands_right,))

            @pl.when(last)
            def _():
                add(p, chip, dst, terms + (lands_left,))

            @pl.when(jnp.logical_not(first) & jnp.logical_not(last))
            def _():
                add(p, chip, dst, terms + (lands_left, lands_right))

            if stream == 1:
                cross(p, chip).start()

    for k in far_first:

        def onward(chip, side):
            pass_on(1, chip, side, 1, (mine_b,))
            if side:
                pass_on(1, chip, side, 0, (mine_a,))
            for p in (0, 2):
                cross(p, chip).wait_recv()
                pass_on(p, chip, side, 0, (mine_a, crossed))
            if not side:
                pass_on(1, chip, side, 0, (mine_a,))

        each(k, onward)

    for k in far_first:

        def finish(chip, side):
            for p in range(3):
                swap(p, chip, a, got_a, 2).wait_send()
                swap(p, chip, b, got_b, 4).wait_send()
                if p != 1 or side == 0:
                    cross(p, chip).wait_send()
                for stream in range(2 if p == 1 else 1):
                    if side == 1:
                        to_right(p, chip, stream).wait_send()
                    elif side == -1:
                        to_left(p, chip, stream).wait_send()

        each(k, finish)


def reduce_grads(sections, n_dp, grads_a, grads_b):
    total, rank = grads_a[0].shape
    width = total // n_dp
    chips = n_dp // 2

    def prepared(grads):
        norm, down, latent, up = grads[2], grads[0], grads[3], grads[1]
        if width % 128:
            up = up.reshape(rank, n_dp, width).transpose(1, 0, 2)
        small = jnp.concatenate([norm.reshape(n_dp, width), latent.reshape(n_dp, rank // n_dp)], axis=1)
        small = jnp.pad(small, ((0, 0), (0, 1024 - small.shape[1]))).reshape(n_dp, 8, 128)
        return down, up, small

    blocks = [
        pltpu.VMEM((chips, width, rank), BF16),
        pltpu.VMEM((chips, rank, width), BF16),
        pltpu.VMEM((chips, 8, 128), F32),
    ]
    down, up, small = pl.pallas_call(
        functools.partial(reduce_kernel, sections, chips),
        out_shape=(
            jax.ShapeDtypeStruct((width, rank), F32),
            jax.ShapeDtypeStruct((rank, width), F32),
            jax.ShapeDtypeStruct((8, 128), F32),
        ),
        in_specs=[pl.BlockSpec(memory_space=pl.ANY)] * 6,
        out_specs=(pl.BlockSpec(memory_space=pltpu.VMEM),) * 3,
        scratch_shapes=blocks * 7 + [pltpu.SemaphoreType.DMA((16, 3, chips))] + blocks[1:2] * 2,
        compiler_params=pltpu.CompilerParams(
            collective_id=1, has_side_effects=True, vmem_limit_bytes=56 * 2**20
        ),
        cost_estimate=pl.CostEstimate(flops=0, bytes_accessed=10**6, transcendentals=0),
        name="reduce_grads",
    )(*prepared(grads_a), *prepared(grads_b))
    flat = small.reshape(1024)
    return flat[:width], down, flat[width : width + rank // n_dp], up


def from_behind(block, axis, distance):
    devices = range(lax.axis_size(axis))
    route = [(i - distance, i) for i in devices if i - distance in devices]
    return lax.ppermute(block, axis, route)


def dot(p, q, contract):
    return lax.dot_general(p, q, (contract, ((), ())), preferred_element_type=F32)


def inner(x, gain, wd, latent_gain):
    xf = x.astype(F32)
    r = lax.rsqrt(jnp.mean(xf * xf, axis=-1, keepdims=True) + 1e-06)
    normed = (xf * r * gain).astype(BF16)
    latent = dot(normed, wd, ((1,), (0,)))
    rl = lax.rsqrt(jnp.mean(latent * latent, axis=-1, keepdims=True) + 1e-06)
    scaled = (latent * rl * latent_gain).astype(BF16)
    return r, normed, latent, rl, scaled


def forward(x, weights):
    gain, wd, latent_gain, wu = weights
    scaled = inner(x, gain, wd, latent_gain)[4]
    return (x.astype(F32) + dot(scaled, wu, ((1,), (0,)))).astype(BF16)


def latent_grads(g, latent, rl, weights):
    gain, wd, latent_gain, wu = weights
    d_scaled = dot(g, wu, ((1,), (1,)))
    d_latent_gain = jnp.sum(d_scaled * latent * rl, axis=0)
    d_hat = d_scaled * latent_gain
    d_latent = rl * (d_hat - latent * (rl * rl * jnp.mean(d_hat * latent, axis=-1, keepdims=True)))
    along = jnp.sum(d_latent * latent, axis=-1, keepdims=True)
    return d_latent.astype(BF16), along, d_latent_gain


def input_grads(x, g, r, d_latent, along, weights):
    gain, wd = weights[:2]
    d_normed = dot(d_latent, wd, ((1,), (1,))).astype(BF16).astype(F32)
    unit = x.astype(F32) * r
    d_gain = jnp.sum(d_normed * unit, axis=0)
    back = g.astype(F32) + r * (d_normed * gain - unit * (along / x.shape[1]))
    return back.astype(BF16), d_gain


def body(
    enter_a, enter_b, cotan_a, cotan_b, saved_a, saved_b, norm_gain, w_down, latent_gain, w_up
):
    sections, n_dp = lax.axis_size("section"), lax.axis_size("dp")
    total, rank = norm_gain.shape[1], latent_gain.shape[1]
    gains = jnp.concatenate([norm_gain[0], latent_gain[0]])
    gains = jnp.pad(gains, (0, -gains.shape[0] % 1024)).reshape(-1, 128)
    owd, owu, mwd, mwu, mgains = gather(sections, n_dp, w_down[0], w_up[0], gains)
    mgains = mgains.reshape(-1)
    own = (norm_gain[0], owd, latent_gain[0], owu)
    mir = (mgains[:total], mwd, mgains[total : total + rank], mwu)

    def first_back(saved, g, weights):
        kept = inner(saved[0, 0], *weights[:3])
        r, normed, latent, rl, scaled = kept
        d_latent, along, d_latent_gain = latent_grads(g, latent, rl, weights)
        back, d_gain = input_grads(saved[0, 0], g, r, d_latent, along, weights)
        return back, (normed, d_latent, scaled, g, d_gain, d_latent_gain)

    def second_back(saved, g, weights, first, kept):
        r, normed, latent, rl, scaled = kept
        d_latent, along, d_latent_gain = latent_grads(g, latent, rl, weights)
        back, d_gain = input_grads(saved[1, 0], g, r, d_latent, along, weights)
        down = dot(first[0], first[1], ((0,), (0,))) + dot(normed, d_latent, ((0,), (0,)))
        up = dot(first[2], first[3], ((0,), (0,))) + dot(scaled, g, ((0,), (0,)))
        small = [(p + q).astype(BF16).astype(F32) for p, q in zip(first[4:], (d_gain, d_latent_gain))]
        return back, (down.astype(BF16), up.astype(BF16), *small)

    back_a, first_a = first_back(saved_a, cotan_a[0], own)
    grad_a = from_behind(back_a, "section", -1)
    back_b, first_b = first_back(saved_b, cotan_b[0], mir)
    grad_b = from_behind(back_b, "section", 1)
    out_a = forward(enter_a[0], own)
    out_b = forward(enter_b[0], mir)
    kept_a = inner(saved_a[1, 0], *own[:3])
    kept_b = inner(saved_b[1, 0], *mir[:3])
    grad_a, grad_b, out_a, out_b, kept_a, kept_b = lax.optimization_barrier(
        (grad_a, grad_b, out_a, out_b, kept_a, kept_b)
    )
    state_a = from_behind(out_a, "section", 1)
    state_b = from_behind(out_b, "section", -1)
    back_a, grads_a = second_back(saved_a, grad_a, own, first_a, kept_a)
    back_b, grads_b = second_back(saved_b, grad_b, mir, first_b, kept_b)

    norm, down, latent, up = reduce_grads(sections, n_dp, grads_a, grads_b)
    state_a, state_b, norm = lax.optimization_barrier((state_a, state_b, norm))
    out_a = forward(state_a, own)
    out_b = forward(state_b, mir)
    return (
        out_a[None],
        out_b[None],
        back_a[None],
        back_b[None],
        norm[None],
        down[None],
        latent[None],
        up[None],
    )


def solution(mesh):
    placed = (
        P("section", "dp", None),
        P("section", "dp", None),
        P("section", "dp", None),
        P("section", "dp", None),
        P(None, "section", "dp", None),
        P(None, "section", "dp", None),
        P("section", None),
        P("section", "dp", None),
        P("section", None),
        P("section", None, "dp"),
    )
    return jax.shard_map(
        body,
        mesh=mesh,
        in_specs=placed,
        out_specs=(
            P("section", "dp", None),
            P("section", "dp", None),
            P("section", "dp", None),
            P("section", "dp", None),
            P("section", "dp"),
            P("section", "dp", None),
            P("section", "dp"),
            P("section", None, "dp"),
        ),
        check_vma=False,
    )
```

```python
import functools

import jax
import jax.numpy as jnp
from jax import lax
from jax.experimental import pallas as pl
from jax.experimental.pallas import tpu as pltpu
from jax.sharding import PartitionSpec as P

TICKS = 2
MESH = pl.DeviceIdType.MESH
BF16 = jnp.bfloat16
F32 = jnp.float32


def place():
    s, d = lax.axis_index("section"), lax.axis_index("dp")
    return s, d, lax.div(d, 2), lax.rem(d, 2)


def greet(sections, chips):
    s, d, z, c = place()
    barrier = pltpu.get_barrier_semaphore()

    def hello(section, index):
        pl.semaphore_signal(barrier, inc=1, device_id=(section, index), device_id_type=MESH)

    hello(sections - 1 - s, d)
    hello(s, d + 1 - 2 * c)

    @pl.when(z > 0)
    def _():
        hello(s, d - 2)

    @pl.when(z < chips - 1)
    def _():
        hello(s, d + 2)

    pl.semaphore_wait(barrier, 2 + jnp.minimum(z, 1) + jnp.minimum(chips - 1 - z, 1))


def down_at(full, e, rows):
    return full.at[pl.ds(pl.multiple_of(e * rows, 16), rows), :]


def up_at(full, e, columns):
    if len(full.shape) == 3:
        return full.at[e]
    return full.at[:, pl.ds(pl.multiple_of(e * columns, 128), columns)]


def remote(src, dst, send, recv, device):
    return pltpu.make_async_remote_copy(
        src_ref=src, dst_ref=dst, send_sem=send, recv_sem=recv, device_id=device, device_id_type=MESH
    )


def gather_kernel(
    sections, chips, wd, wu, gains, owd, owu, mwd, mwu, mgains, sems, local_sems, gain_sems
):
    s, d, z, c = place()
    width = wd.shape[0]
    mirror = (sections - 1 - s, d)
    sibling = (s, d + 1 - 2 * c)
    right, left = (s, d + 2), (s, d - 2)
    greet(sections, chips)

    def slot(full, p, chip, core):
        return (down_at, up_at)[p](full[p], chip * 2 + core, width)

    own, mir, shard = (owd, owu), (mwd, mwu), (wd, wu)

    def at(kind, p, chip):
        return sems.at[kind, p, chip]

    def line_copy(p, chip, src, kind, device):
        return remote(src, slot(own, p, chip, c), at(kind, p, chip), at(0, p, chip), device)

    def sibling_copy(p, chip, src):
        return remote(src, slot(own, p, chip, c), at(3, p, chip), at(4, p, chip), sibling)

    def mirror_copy(p, chip, src):
        return remote(src, slot(mir, p, chip, c), at(5, p, chip), at(6, p, chip), mirror)

    def mirror_sibling_copy(p, chip):
        block = slot(mir, p, chip, c)
        return remote(block, block, at(7, p, chip), at(8, p, chip), sibling)

    def mirror_line_copy(chip, toward):
        kind, device = (9, right) if toward == 1 else (11, left)
        block = slot(mir, 1, chip, c)
        return remote(block, block, at(kind, 1, chip), at(kind + 1, 1, chip), device)

    def crosses(chip):
        return (chip > 0) & (chip < chips - 1)

    gain_copy = remote(gains, mgains, gain_sems.at[0], gain_sems.at[1], mirror)
    for p in range(2):
        pltpu.make_async_copy(shard[p], slot(own, p, z, c), local_sems.at[p]).start()

        @pl.when(z < chips - 1)
        def _():
            line_copy(p, z, shard[p], 1, right).start()

        @pl.when(z > 0)
        def _():
            line_copy(p, z, shard[p], 2, left).start()

        mirror_copy(p, z, shard[p]).start()
        sibling_copy(p, z, shard[p]).start()
    gain_copy.start()

    def pass_mirror(k):
        for p in range(2):
            for toward, chip in ((1, z - k), (-1, z + k))[: 1 if k == 0 else 2]:

                @pl.when((chip >= 0) & (chip < chips))
                def _():
                    if p == 0 or k == 0:
                        mirror_copy(p, chip, slot(mir, p, chip, c)).wait_recv()
                    else:

                        @pl.when(crosses(chip))
                        def _():
                            mirror_copy(p, chip, slot(mir, p, chip, c)).wait_recv()

                        @pl.when(jnp.logical_not(crosses(chip)))
                        def _():
                            mirror_line_copy(chip, toward).wait_recv()

                    if p == 1:

                        @pl.when((chip == 0) & (z < chips - 1))
                        def _():
                            mirror_line_copy(chip, 1).start()

                        @pl.when((chip == chips - 1) & (z > 0))
                        def _():
                            mirror_line_copy(chip, -1).start()

                    mirror_sibling_copy(p, chip).start()

    for k in range(1, chips):
        for p in range(2):

            @pl.when(z - k >= 0)
            def _():
                block = slot(own, p, z - k, c)
                line_copy(p, z - k, block, 1, right).wait_recv()

                @pl.when(z < chips - 1)
                def _():
                    line_copy(p, z - k, block, 1, right).start()

                if p == 0:
                    mirror_copy(p, z - k, block).start()
                else:

                    @pl.when(crosses(z - k))
                    def _():
                        mirror_copy(p, z - k, block).start()

                sibling_copy(p, z - k, block).start()

            @pl.when(z + k < chips)
            def _():
                block = slot(own, p, z + k, c)
                line_copy(p, z + k, block, 2, left).wait_recv()

                @pl.when(z > 0)
                def _():
                    line_copy(p, z + k, block, 2, left).start()

                if p == 0:
                    mirror_copy(p, z + k, block).start()
                else:

                    @pl.when(crosses(z + k))
                    def _():
                        mirror_copy(p, z + k, block).start()

                sibling_copy(p, z + k, block).start()

        pass_mirror(k - 1)
    pass_mirror(chips - 1)

    for p in range(2):
        pltpu.make_async_copy(shard[p], slot(own, p, z, c), local_sems.at[p]).wait()
        for chip in range(chips):
            theirs = slot(own, p, chip, 1 - c)
            remote(theirs, theirs, at(3, p, chip), at(4, p, chip), sibling).wait()
            if p == 0:
                mirror_copy(p, chip, slot(own, p, chip, c)).wait_send()
            else:

                @pl.when(crosses(chip) | (chip == z))
                def _():
                    mirror_copy(p, chip, slot(own, p, chip, c)).wait_send()

            theirs = slot(mir, p, chip, 1 - c)
            remote(theirs, theirs, at(7, p, chip), at(8, p, chip), sibling).wait()

            @pl.when((chip <= z) & (z < chips - 1))
            def _():
                line_copy(p, chip, slot(own, p, chip, c), 1, right).wait_send()

            @pl.when((chip >= z) & (z > 0))
            def _():
                line_copy(p, chip, slot(own, p, chip, c), 2, left).wait_send()

    @pl.when(z < chips - 1)
    def _():
        mirror_line_copy(0, 1).wait_send()

    @pl.when(z > 0)
    def _():
        mirror_line_copy(chips - 1, -1).wait_send()

    gain_copy.wait()


def gather(sections, n_dp, wd, wu, gains):
    width, rank = wd.shape
    up_shape = (rank, n_dp * width) if width % 128 == 0 else (n_dp, rank, width)
    down = jax.ShapeDtypeStruct((n_dp * width, rank), wd.dtype)
    up = jax.ShapeDtypeStruct(up_shape, wu.dtype)
    chips = n_dp // 2
    owd, owu, mwd, mwu, mgains = pl.pallas_call(
        functools.partial(gather_kernel, sections, chips),
        out_shape=(down, up, down, up, jax.ShapeDtypeStruct(gains.shape, gains.dtype)),
        in_specs=[pl.BlockSpec(memory_space=pl.ANY)] * 3,
        out_specs=(pl.BlockSpec(memory_space=pl.ANY),) * 5,
        scratch_shapes=[
            pltpu.SemaphoreType.DMA((13, 2, chips)),
            pltpu.SemaphoreType.DMA((2,)),
            pltpu.SemaphoreType.DMA((2,)),
        ],
        compiler_params=pltpu.CompilerParams(
            collective_id=0, has_side_effects=True, vmem_limit_bytes=56 * 2**20
        ),
        name="gather_weights",
    )(wd, wu, gains)

    def whole(v):
        return v if v.ndim == 2 else v.transpose(1, 0, 2).reshape(rank, n_dp * width)

    return owd, whole(owu), mwd, whole(mwu), mgains


def reduce_kernel(sections, chips, ad, au, asm, bd, bu, bsm, od, ou, osm, *scratch):
    s, d, z, c = place()
    width = od.shape[0]
    mirror = (sections - 1 - s, d)
    sibling = (s, d + 1 - 2 * c)
    right, left = (s, d + 2), (s, d - 2)
    mine_a, mine_b, got_a, got_b, crossed, from_left, from_right = (
        scratch[3 * i : 3 * i + 3] for i in range(7)
    )
    sems, left_b, right_b = scratch[21:24]
    a, b, out = (ad, au, asm), (bd, bu, bsm), (od, ou, osm)

    def part(full, p, chip, core):
        e = chip * 2 + core
        if p == 0:
            return down_at(full[0], e, width)
        if p == 1:
            return up_at(full[1], e, width)
        return full[2].at[e]

    def at(kind, p, chip):
        return sems.at[kind, p, chip]

    def load(p, chip, full, mine, kind):
        return pltpu.make_async_copy(part(full, p, chip, c), mine[p].at[chip], at(kind, p, chip))

    def swap(p, chip, full, got, kind):
        return remote(
            part(full, p, chip, 1 - c), got[p].at[chip], at(kind, p, chip), at(kind + 1, p, chip), sibling
        )

    def cross(p, chip):
        return remote(mine_b[p].at[chip], crossed[p].at[chip], at(6, p, chip), at(7, p, chip), mirror)

    def to_right(p, chip, stream=0):
        kind, mine, lands = ((8, mine_a, from_left), (12, mine_b, {1: left_b}))[stream]
        return remote(
            mine[p].at[chip], lands[p].at[chip], at(kind, p, chip), at(kind + 1, p, chip), right
        )

    def to_left(p, chip, stream=0):
        kind, mine, lands = ((10, mine_a, from_right), (14, mine_b, {1: right_b}))[stream]
        return remote(
            mine[p].at[chip], lands[p].at[chip], at(kind, p, chip), at(kind + 1, p, chip), left
        )

    def add(p, chip, dst, terms):
        rows = terms[0][p].shape[1]
        step = rows if p == 2 else rows // 8 if rows % 128 == 0 else rows // 7

        def body(i, carry):
            at_rows = pl.ds(pl.multiple_of(i * step, 8 if p == 2 else 16), step)
            total = terms[0][p][chip, at_rows, :].astype(F32)
            for term in terms[1:]:
                total = total + term[p][chip, at_rows, :].astype(F32)
            if dst is out:
                dst[p][at_rows, :] = total
            else:
                dst[p][chip, at_rows, :] = total.astype(dst[p].dtype)
            return carry

        lax.fori_loop(0, rows // step, body, 0)

    def each(k, do):
        if k == 0:
            do(z, 0)
        else:

            @pl.when(z + k < chips)
            def _():
                do(z + k, 1)

            @pl.when(z - k >= 0)
            def _():
                do(z - k, -1)

    greet(sections, chips)
    far_first = list(range(chips - 1, -1, -1))
    for full, mine, got, kind, local in ((b, mine_b, got_b, 4, 1), (a, mine_a, got_a, 2, 0)):
        for k in far_first:

            def begin(chip, side):
                for p in range(3):
                    swap(p, chip, full, got, kind).start()
                    load(p, chip, full, mine, local).start()

            each(k, begin)
    for full, mine, got, kind, local in ((b, mine_b, got_b, 4, 1), (a, mine_a, got_a, 2, 0)):
        for k in far_first:

            def pair(chip, side):
                for p in range(3):
                    swap(p, chip, full, got, kind).wait_recv()
                    load(p, chip, full, mine, local).wait()
                    add(p, chip, mine, (mine, got))
                    if local == 1 and p != 1:
                        cross(p, chip).start()

            each(k, pair)

    def pass_on(p, chip, side, stream, terms):
        mine = (mine_a, mine_b)[stream]
        lands_left = (from_left, {1: left_b})[stream]
        lands_right = (from_right, {1: right_b})[stream]
        first, last = z == 0, z == chips - 1
        if side == 1:

            @pl.when(jnp.logical_not(first))
            def _():
                to_right(p, chip, stream).wait_recv()
                add(p, chip, mine, terms + (lands_left,))

            if len(terms) > 1:

                @pl.when(first)
                def _():
                    add(p, chip, mine, terms)

            to_right(p, chip, stream).start()
        elif side == -1:

            @pl.when(jnp.logical_not(last))
            def _():
                to_left(p, chip, stream).wait_recv()
                add(p, chip, mine, terms + (lands_right,))

            if len(terms) > 1:

                @pl.when(last)
                def _():
                    add(p, chip, mine, terms)

            to_left(p, chip, stream).start()
        else:

            @pl.when(jnp.logical_not(first))
            def _():
                to_right(p, chip, stream).wait_recv()

            @pl.when(jnp.logical_not(last))
            def _():
                to_left(p, chip, stream).wait_recv()

            if stream == 0 and p == 1:
                cross(p, chip).wait_recv()
                terms = terms + (crossed,)
            dst = (out, mine_b)[stream]

            @pl.when(first)
            def _():
                add(p, chip, dst, terms + (lands_right,))

            @pl.when(last)
            def _():
                add(p, chip, dst, terms + (lands_left,))

            @pl.when(jnp.logical_not(first) & jnp.logical_not(last))
            def _():
                add(p, chip, dst, terms + (lands_left, lands_right))

            if stream == 1:
                cross(p, chip).start()

    for k in far_first:

        def onward(chip, side):
            pass_on(1, chip, side, 1, (mine_b,))
            if side:
                pass_on(1, chip, side, 0, (mine_a,))
            for p in (0, 2):
                cross(p, chip).wait_recv()
                pass_on(p, chip, side, 0, (mine_a, crossed))
            if not side:
                pass_on(1, chip, side, 0, (mine_a,))

        each(k, onward)

    for k in far_first:

        def finish(chip, side):
            for p in range(3):
                swap(p, chip, a, got_a, 2).wait_send()
                swap(p, chip, b, got_b, 4).wait_send()
                if p != 1 or side == 0:
                    cross(p, chip).wait_send()
                for stream in range(2 if p == 1 else 1):
                    if side == 1:
                        to_right(p, chip, stream).wait_send()
                    elif side == -1:
                        to_left(p, chip, stream).wait_send()

        each(k, finish)


def reduce_grads(sections, n_dp, grads_a, grads_b):
    total, rank = grads_a[0].shape
    width = total // n_dp
    chips = n_dp // 2

    def prepared(grads):
        norm, down, latent, up = grads[2], grads[0], grads[3], grads[1]
        if width % 128:
            up = up.reshape(rank, n_dp, width).transpose(1, 0, 2)
        small = jnp.concatenate([norm.reshape(n_dp, width), latent.reshape(n_dp, rank // n_dp)], axis=1)
        small = jnp.pad(small, ((0, 0), (0, 1024 - small.shape[1]))).reshape(n_dp, 8, 128)
        return down, up, small

    blocks = [
        pltpu.VMEM((chips, width, rank), BF16),
        pltpu.VMEM((chips, rank, width), BF16),
        pltpu.VMEM((chips, 8, 128), F32),
    ]
    down, up, small = pl.pallas_call(
        functools.partial(reduce_kernel, sections, chips),
        out_shape=(
            jax.ShapeDtypeStruct((width, rank), F32),
            jax.ShapeDtypeStruct((rank, width), F32),
            jax.ShapeDtypeStruct((8, 128), F32),
        ),
        in_specs=[pl.BlockSpec(memory_space=pl.ANY)] * 6,
        out_specs=(pl.BlockSpec(memory_space=pltpu.VMEM),) * 3,
        scratch_shapes=blocks * 7 + [pltpu.SemaphoreType.DMA((16, 3, chips))] + blocks[1:2] * 2,
        compiler_params=pltpu.CompilerParams(
            collective_id=1, has_side_effects=True, vmem_limit_bytes=56 * 2**20
        ),
        cost_estimate=pl.CostEstimate(flops=0, bytes_accessed=10**6, transcendentals=0),
        name="reduce_grads",
    )(*prepared(grads_a), *prepared(grads_b))
    flat = small.reshape(1024)
    return flat[:width], down, flat[width : width + rank // n_dp], up


def from_behind(block, axis, distance):
    devices = range(lax.axis_size(axis))
    route = [(i - distance, i) for i in devices if i - distance in devices]
    return lax.ppermute(block, axis, route)


def dot(p, q, contract):
    return lax.dot_general(p, q, (contract, ((), ())), preferred_element_type=F32)


def inner(x, gain, wd, latent_gain):
    xf = x.astype(F32)
    r = lax.rsqrt(jnp.mean(xf * xf, axis=-1, keepdims=True) + 1e-06)
    normed = (xf * r * gain).astype(BF16)
    latent = dot(normed, wd, ((1,), (0,)))
    rl = lax.rsqrt(jnp.mean(latent * latent, axis=-1, keepdims=True) + 1e-06)
    scaled = (latent * rl * latent_gain).astype(BF16)
    return r, normed, latent, rl, scaled


def forward(x, weights):
    gain, wd, latent_gain, wu = weights
    scaled = inner(x, gain, wd, latent_gain)[4]
    return (x.astype(F32) + dot(scaled, wu, ((1,), (0,)))).astype(BF16)


def latent_grads(g, latent, rl, weights):
    gain, wd, latent_gain, wu = weights
    d_scaled = dot(g, wu, ((1,), (1,)))
    d_latent_gain = jnp.sum(d_scaled * latent * rl, axis=0)
    d_hat = d_scaled * latent_gain
    d_latent = rl * (d_hat - latent * (rl * rl * jnp.mean(d_hat * latent, axis=-1, keepdims=True)))
    along = jnp.sum(d_latent * latent, axis=-1, keepdims=True)
    return d_latent.astype(BF16), along, d_latent_gain


def input_grads(x, g, r, d_latent, along, weights):
    gain, wd = weights[:2]
    d_normed = dot(d_latent, wd, ((1,), (1,))).astype(BF16).astype(F32)
    unit = x.astype(F32) * r
    d_gain = jnp.sum(d_normed * unit, axis=0)
    back = g.astype(F32) + r * (d_normed * gain - unit * (along / x.shape[1]))
    return back.astype(BF16), d_gain


def body(
    enter_a, enter_b, cotan_a, cotan_b, saved_a, saved_b, norm_gain, w_down, latent_gain, w_up
):
    sections, n_dp = lax.axis_size("section"), lax.axis_size("dp")
    total, rank = norm_gain.shape[1], latent_gain.shape[1]
    gains = jnp.concatenate([norm_gain[0], latent_gain[0]])
    gains = jnp.pad(gains, (0, -gains.shape[0] % 1024)).reshape(-1, 128)
    owd, owu, mwd, mwu, mgains = gather(sections, n_dp, w_down[0], w_up[0], gains)
    mgains = mgains.reshape(-1)
    own = (norm_gain[0], owd, latent_gain[0], owu)
    mir = (mgains[:total], mwd, mgains[total : total + rank], mwu)

    def normed_of(saved, gain):
        xf = saved[:, 0].astype(F32)
        r = lax.rsqrt(jnp.mean(xf * xf, axis=-1, keepdims=True) + 1e-06)
        return (xf * r * gain).astype(BF16).reshape(-1, total)

    def first_back(saved, g, weights):
        kept = inner(saved[0, 0], *weights[:3])
        r, normed, latent, rl, scaled = kept
        d_latent, along, d_latent_gain = latent_grads(g, latent, rl, weights)
        back, d_gain = input_grads(saved[0, 0], g, r, d_latent, along, weights)
        return back, (d_latent, scaled, g, d_gain, d_latent_gain)

    def second_back(saved, g, weights, first, kept):
        r, normed, latent, rl, scaled = kept
        d_latent, along, d_latent_gain = latent_grads(g, latent, rl, weights)
        back, d_gain = input_grads(saved[1, 0], g, r, d_latent, along, weights)
        both = jnp.concatenate([first[0], d_latent])
        down = dot(normed_of(saved, weights[0]), both, ((0,), (0,)))
        up = dot(first[1], first[2], ((0,), (0,))) + dot(scaled, g, ((0,), (0,)))
        small = [(p + q).astype(BF16).astype(F32) for p, q in zip(first[3:], (d_gain, d_latent_gain))]
        return back, (down.astype(BF16), up.astype(BF16), *small)

    back_a, first_a = first_back(saved_a, cotan_a[0], own)
    grad_a = from_behind(back_a, "section", -1)
    back_b, first_b = first_back(saved_b, cotan_b[0], mir)
    grad_b = from_behind(back_b, "section", 1)
    out_a = forward(enter_a[0], own)
    out_b = forward(enter_b[0], mir)
    kept_a = inner(saved_a[1, 0], *own[:3])
    kept_b = inner(saved_b[1, 0], *mir[:3])
    grad_a, grad_b, out_a, out_b, kept_a, kept_b = lax.optimization_barrier(
        (grad_a, grad_b, out_a, out_b, kept_a, kept_b)
    )
    state_a = from_behind(out_a, "section", 1)
    state_b = from_behind(out_b, "section", -1)
    back_a, grads_a = second_back(saved_a, grad_a, own, first_a, kept_a)
    back_b, grads_b = second_back(saved_b, grad_b, mir, first_b, kept_b)

    norm, down, latent, up = reduce_grads(sections, n_dp, grads_a, grads_b)
    state_a, state_b, norm = lax.optimization_barrier((state_a, state_b, norm))
    out_a = forward(state_a, own)
    out_b = forward(state_b, mir)
    return (
        out_a[None],
        out_b[None],
        back_a[None],
        back_b[None],
        norm[None],
        down[None],
        latent[None],
        up[None],
    )


def solution(mesh):
    placed = (
        P("section", "dp", None),
        P("section", "dp", None),
        P("section", "dp", None),
        P("section", "dp", None),
        P(None, "section", "dp", None),
        P(None, "section", "dp", None),
        P("section", None),
        P("section", "dp", None),
        P("section", None),
        P("section", None, "dp"),
    )
    return jax.shard_map(
        body,
        mesh=mesh,
        in_specs=placed,
        out_specs=(
            P("section", "dp", None),
            P("section", "dp", None),
            P("section", "dp", None),
            P("section", "dp", None),
            P("section", "dp"),
            P("section", "dp", None),
            P("section", "dp"),
            P("section", None, "dp"),
        ),
        check_vma=False,
    )
```
